32 devices in a mesh: pairs: 4 (over y, x), rows: 2 (over core), cols: 4 (over z).
Axes of the slice: x: 2, y: 2, z: 4, core: 2. Of those that a mesh axis runs over, the one named last changes fastest.
Arguments:
- frame_one: bfloat16 [4, 1536, 128], P('pairs', 'rows'), may hold values from -16 to 16
- frame_two: bfloat16 [4, 1536, 128], P('pairs', ('rows', 'cols')), may hold values from -16 to 16
- weight: bfloat16 [128, 128], replicated, may hold values from -0.5 to 0.5
- flow_cot: float32 [4, 2, 1536], P('pairs', None, 'rows'), may hold values from -60 to 60
Outputs:
- flow: float32 [4, 2, 1536], P('pairs', None, 'rows')
- grad_one: float32 [4, 1536, 128], P('pairs', 'rows')
- grad_two: float32 [4, 1536, 128], P('pairs', ('rows', 'cols'))
- grad_w: float32 [128, 128], replicated
The draws below stay inside these ranges and needn't reach their ends.
All inputs are finite; a program needn't handle non-finite values.
Results may differ from the reference program's by a relative error of at most 0.002.
The reference program's roundings to bfloat16 on the way (of `slope`) count: a program that leaves them out, or rounds other values in their place, can miss the bound.
Values may be sent and summed in bfloat16 or wider, within the bound.
A program may use at most 64 MiB of HBM per device.

```python
import math
import jax
import jax.numpy as jnp
from jax import lax

C = 128
IMG_W = 128
POS = 1536
PAIRS = 4


def frame_base(key, spread):
    normal_part = jnp.clip(jax.random.normal(jax.random.fold_in(key, 1), (PAIRS, POS, C), jnp.float32), -6.0, 6.0)
    return spread * normal_part


def draw_frame_two(key, part):
    shared = frame_base(key, 1.6)
    return shared.astype(jnp.bfloat16)


def draw_frame_one(key, part):
    own_key = jax.random.fold_in(key, 3)
    own = frame_base(own_key, 1.6)
    return own.astype(jnp.bfloat16)


def levels(key, shape, pieces, least, largest):
    def one(position, parts):
        steps = jax.random.uniform(jax.random.fold_in(jax.random.fold_in(key, 6), position), (parts,), jnp.float32, least / len(pieces), largest / len(pieces))
        return jnp.repeat(jnp.exp(steps), shape[position] // parts).reshape((-1,) + (1,) * (len(shape) - position - 1))

    factor_of = one(*pieces[0])
    for cut in pieces[1:]:
        factor_of = factor_of * one(*cut)
    return factor_of


def centred(key, extent, scale, bound, pieces=(), kind=jnp.bfloat16):
    values = jax.random.normal(key, extent, jnp.float32) * scale
    if len(pieces) > 0:
        values = levels(key, extent, pieces, -0.22, 0.18) * values
    return jnp.clip(values, min=-bound, max=bound).astype(kind)


def setup_inputs(seed: int = 0) -> dict:
    streams_of = jax.random.split(jax.random.key(seed), 5)
    return {
        "frame_one": draw_frame_one(jax.random.fold_in(streams_of[4], 71), 0),
        "frame_two": draw_frame_two(jax.random.fold_in(streams_of[4], 71), 0),
        "weight": centred(streams_of[2], (C, C), C ** -0.5, 0.5),
        "flow_cot": centred(streams_of[3], (PAIRS, 2, POS), 10.0, 60.0, ((0, 4), (2, 2)), jnp.float32),
    }


coord_unit = 0.0625

def coords(index):
    return jnp.stack([(index % IMG_W).astype(jnp.float32), (index // IMG_W).astype(jnp.float32)]) * coord_unit

def one_pair(x_one, x_two, cot, weight):
    scale = 1.0 / math.sqrt(C)
    qblk = min(512, POS)
    nblk = POS // qblk
    key_coords = coords(jnp.arange(POS, dtype=jnp.int32))
    proj_one = jnp.dot(x_one, weight, preferred_element_type=jnp.float32).astype(jnp.bfloat16)
    proj_two = jnp.dot(x_two, weight, preferred_element_type=jnp.float32).astype(jnp.bfloat16)
    query_coords = coords(jnp.arange(POS, dtype=jnp.int32))
    feat_blocks = proj_one.reshape(nblk, qblk, C)
    cot_blocks = cot.reshape(2, nblk, qblk).transpose(1, 0, 2)
    qc_blocks = query_coords.reshape(2, nblk, qblk).transpose(1, 0, 2)

    def step(acc, blk):
        fq, gq, qc = blk
        scores = jnp.dot(fq, proj_two.T, preferred_element_type=jnp.float32) * scale
        top = lax.optimization_barrier(jnp.max(scores, axis=1))
        expo = jnp.exp(scores - top[:, None])
        total = lax.optimization_barrier(jnp.sum(expo, axis=1))
        sum_x = jnp.dot(expo, key_coords[0], precision=lax.Precision.HIGHEST)
        sum_y = jnp.dot(expo, key_coords[1], precision=lax.Precision.HIGHEST)
        mean_x = sum_x / total
        mean_y = sum_y / total
        flow = jnp.stack([mean_x, mean_y]) - qc
        offset = gq[0] * mean_x + gq[1] * mean_y
        inner = gq[0][:, None] * key_coords[0][None, :] + gq[1][:, None] * key_coords[1][None, :]
        prob = jnp.exp(scores - top[:, None]) / total[:, None]
        slope = (prob * (inner - offset[:, None])).astype(jnp.bfloat16)
        grad_q = jnp.dot(slope, proj_two, preferred_element_type=jnp.float32) * scale
        acc = acc + jnp.dot(slope.T, fq, preferred_element_type=jnp.float32) * scale
        return (acc, (flow, grad_q))
    feat_two_grad, outs = lax.scan(step, jnp.zeros((POS, C), jnp.float32), (feat_blocks, cot_blocks, qc_blocks))
    flow = outs[0].transpose(1, 0, 2).reshape(2, POS)
    feat_one_grad = outs[1].reshape(POS, C)
    grad_one = jnp.dot(feat_one_grad.astype(jnp.bfloat16), weight.T, preferred_element_type=jnp.float32)
    grad_two = jnp.dot(feat_two_grad.astype(jnp.bfloat16), weight.T, preferred_element_type=jnp.float32)
    term = jnp.dot(x_one.astype(jnp.float32).T, feat_one_grad, precision=lax.Precision.HIGHEST)
    term = term + jnp.dot(x_two.astype(jnp.float32).T, feat_two_grad, precision=lax.Precision.HIGHEST)
    return (flow, grad_one, grad_two, term)

def reference(frame_one, frame_two, weight, flow_cot):
    flows = []
    ones = []
    twos = []
    grad_w = jnp.zeros((C, C), jnp.float32)
    for pair in range(PAIRS):
        flow, grad_one, grad_two, term = one_pair(frame_one[pair], frame_two[pair], flow_cot[pair], weight)
        flows.append(flow)
        ones.append(grad_one)
        twos.append(grad_two)
        grad_w = grad_w + term
    grad_w = grad_w / math.sqrt(PAIRS * POS)
    return (jnp.stack(flows), jnp.stack(ones), jnp.stack(twos), grad_w)
```

```python
import functools
import math

import jax
import jax.numpy as jnp
from jax import lax
from jax.experimental import pallas as pl
from jax.experimental.pallas import tpu as pltpu
from jax.sharding import PartitionSpec as P

IMG_W = 128
MESH = pl.DeviceIdType.MESH


coord_unit = 0.0625


def coords(index):
    return (
        jnp.stack([(index % IMG_W).astype(jnp.float32), (index // IMG_W).astype(jnp.float32)])
        * coord_unit
    )


def slopes(feat_q, feat_k, coord_k, top, total, cot_x, cot_y, offset, scale):
    scores = jnp.dot(feat_q, feat_k.T, preferred_element_type=jnp.float32) * scale
    prob = jnp.exp(scores - top[:, None]) / total[:, None]
    inner = cot_x[:, None] * coord_k[0][None, :] + cot_y[:, None] * coord_k[1][None, :]
    return (prob * (inner - offset[:, None])).astype(jnp.bfloat16)


def lead_product(left, right, highest):
    if highest:
        return lax.dot_general(
            left,
            right,
            (((0,), (0,)), ((), ())),
            precision=lax.Precision.HIGHEST,
            preferred_element_type=jnp.float32,
        )
    return lax.dot_general(
        left, right, (((0,), (0,)), ((), ())), preferred_element_type=jnp.float32
    )


def shards(frame_one, frame_two, weight, flow_cot):
    chan = weight.shape[0]
    scale = 1.0 / math.sqrt(chan)
    qrows = frame_one.shape[1]
    krows = frame_two.shape[1]
    nrows = lax.axis_size("rows")
    ncols = lax.axis_size("cols")
    row_id = lax.axis_index("rows")
    col_id = lax.axis_index("cols")
    x_one = frame_one[0]
    x_two = frame_two[0]
    cot = flow_cot[0]
    feat_one = jnp.dot(x_one, weight, preferred_element_type=jnp.float32).astype(jnp.bfloat16)
    feat_two = jnp.dot(x_two, weight, preferred_element_type=jnp.float32).astype(jnp.bfloat16)
    query_coords = coords(row_id * qrows + jnp.arange(qrows, dtype=jnp.int32))
    gathered = lax.all_gather(feat_two, "rows", axis=0, tiled=True)
    kcol = gathered.shape[0]
    width = min(512, kcol)
    nblk = kcol // width
    local = jnp.arange(kcol, dtype=jnp.int32)
    key_index = (local // krows * ncols + col_id) * krows + local % krows
    key_coords = coords(key_index)
    key_blocks = gathered.reshape(nblk, width, chan)
    coord_blocks = key_coords.reshape(2, nblk, width).transpose(1, 0, 2)

    def forward(carry, blk):
        top, total, sum_x, sum_y = carry
        block_keys, block_coords = blk
        scores = jnp.dot(feat_one, block_keys.T, preferred_element_type=jnp.float32) * scale
        new_top = jnp.maximum(top, jnp.max(scores, axis=1))
        shrink = jnp.exp(top - new_top)
        expo = jnp.exp(scores - new_top[:, None])
        total = total * shrink + jnp.sum(expo, axis=1)
        sum_x = sum_x * shrink + jnp.dot(expo, block_coords[0], precision=lax.Precision.HIGHEST)
        sum_y = sum_y * shrink + jnp.dot(expo, block_coords[1], precision=lax.Precision.HIGHEST)
        return ((new_top, total, sum_x, sum_y), None)

    zeros_q = jnp.zeros((qrows,), jnp.float32)
    start_carry = (jnp.full((qrows,), -1e30, jnp.float32), zeros_q, zeros_q, zeros_q)
    (top, total, sum_x, sum_y), _ = lax.scan(forward, start_carry, (key_blocks, coord_blocks))
    peak = lax.pmax(top, "cols")
    shrink = jnp.exp(top - peak)
    total, sum_x, sum_y = lax.psum((total * shrink, sum_x * shrink, sum_y * shrink), "cols")
    top = peak
    mean_x = sum_x / total
    mean_y = sum_y / total
    flow = jnp.stack([mean_x, mean_y]) - query_coords
    cot_x = cot[0]
    cot_y = cot[1]
    offset = cot_x * mean_x + cot_y * mean_y

    def backward(acc, blk):
        block_keys, block_coords = blk
        slope = slopes(feat_one, block_keys, block_coords, top, total, cot_x, cot_y, offset, scale)
        acc = acc + jnp.dot(slope, block_keys, preferred_element_type=jnp.float32) * scale
        return (acc, lead_product(slope, feat_one, False) * scale)

    part_one, terms = lax.scan(
        backward, jnp.zeros((qrows, chan), jnp.float32), (key_blocks, coord_blocks)
    )
    feat_two_grad = lax.psum_scatter(
        terms.reshape(kcol, chan), "rows", scatter_dimension=0, tiled=True
    )
    feat_one_grad = lax.psum(part_one, "cols")
    contract = (((1,), (1,)), ((), ()))
    grad_one = lax.dot_general(
        feat_one_grad.astype(jnp.bfloat16), weight, contract, preferred_element_type=jnp.float32
    )
    grad_two = lax.dot_general(
        feat_two_grad.astype(jnp.bfloat16), weight, contract, preferred_element_type=jnp.float32
    )
    term = lead_product(x_one.astype(jnp.float32), part_one, True) + lead_product(
        x_two.astype(jnp.float32), feat_two_grad, True
    )
    npairs = lax.axis_size("pairs") * frame_one.shape[0]
    grad_w = lax.psum(term, ("pairs", "rows", "cols")) / math.sqrt(npairs * qrows * nrows)
    return (flow[None], grad_one[None], grad_two[None], grad_w)


def pieces(value):
    high = value.astype(jnp.bfloat16)
    rest = value - high.astype(jnp.float32)
    mid = rest.astype(jnp.bfloat16)
    low = (rest - mid.astype(jnp.float32)).astype(jnp.bfloat16)
    return high, mid, low


def last_dims(left, right):
    return lax.dot_general(
        left, right, (((1,), (1,)), ((), ())), preferred_element_type=jnp.float32
    )


def fused(
    npairs, ncols,
    x1_ref, x2_ref, w_ref, cot_ref,
    flow_ref, g1_ref, g2_ref, gw_ref,
    x2all, p1s, score, slope, left, table, two_out, two_in, terms, blocks,
    z_send, z_recv, s_send, s_recv, t_send, t_recv, b_send, b_recv,
):
    qrows, chan = x1_ref.shape[1:]
    krows = x2_ref.shape[1]
    keys = x2all.shape[0]
    chip = 2 * krows
    part = chan // ncols
    scale = 1.0 / math.sqrt(chan)
    pair = lax.axis_index("pairs")
    row = lax.axis_index("rows")
    col = lax.axis_index("cols")
    twin = 1 - row
    orders = [1] + [k for k in range(ncols - 1, 1, -1)]

    def peer(dp, dr, dc):
        return (lax.rem(pair + dp, npairs), lax.rem(row + dr, 2), lax.rem(col + dc, ncols))

    group = [(dp, dr) for dr in range(2) for dp in range(npairs) if (dp, dr) != (0, 0)]
    barrier = pltpu.get_barrier_semaphore()
    for dc in range(1, ncols):
        pl.semaphore_signal(barrier, inc=1, device_id=peer(0, 0, dc), device_id_type=MESH)
    for dp, dr in group:
        pl.semaphore_signal(barrier, inc=1, device_id=peer(dp, dr, 0), device_id_type=MESH)
    pl.semaphore_wait(barrier, ncols - 1 + len(group))

    def place(c, r):
        return pl.ds(pl.multiple_of(c * chip + r * krows, 64), krows)

    own = place(col, row)
    sends = []

    def send(src, dst, ssem, rsem, device):
        copy = pltpu.make_async_remote_copy(
            src_ref=src, dst_ref=dst, send_sem=ssem, recv_sem=rsem,
            device_id=device, device_id_type=MESH,
        )
        copy.start()
        sends.append(copy)
        return copy

    twin_copies = {0: send(x2_ref.at[0], x2all.at[own], s_send.at[0], s_recv.at[0], peer(0, 1, 0))}
    z_copies = {}
    for k in orders:
        z_copies[k] = send(
            x2_ref.at[0], x2all.at[own], z_send.at[k], z_recv.at[k], peer(0, 0, k)
        )

    weight = w_ref[...]
    x2all[own, :] = x2_ref[0]
    x_one = x1_ref[0]
    p1 = jnp.dot(x_one, weight, preferred_element_type=jnp.float32).astype(jnp.bfloat16)
    p1s[...] = p1
    pick = (
        lax.broadcasted_iota(jnp.int32, (part, chan), 1)
        == lax.broadcasted_iota(jnp.int32, (part, chan), 0) + part * col
    ).astype(jnp.float32)
    wt = weight.astype(jnp.float32).T
    proj = jnp.concatenate([wt, pick], axis=0).astype(jnp.bfloat16)
    x_one_t = last_dims(pick.astype(jnp.bfloat16), x_one).astype(jnp.bfloat16)

    def matched(best, c, r):
        at = place(c, r)
        feat = jnp.dot(x2all[at, :], weight, preferred_element_type=jnp.float32)
        values = last_dims(feat.astype(jnp.bfloat16), p1s[...])
        score[at, :] = values
        return jnp.maximum(best, jnp.max(values.reshape(krows // 8, 8, qrows), axis=0))

    def lefts(c):
        at = pl.ds(pl.multiple_of(c * chip, 128), chip)
        left[:, at] = last_dims(proj, x2all[at, :]).astype(jnp.bfloat16)

    best = jnp.full((8, qrows), -jnp.inf, jnp.float32)
    best = matched(best, col, row)
    twin_copies[0].wait_recv()
    best = matched(best, col, twin)
    lefts(col)
    for k in orders:
        source = lax.rem(col + ncols - k, ncols)
        at = place(source, row)
        z_copies[k].wait_recv()
        twin_copies[k] = send(
            x2all.at[at], x2all.at[at], s_send.at[k], s_recv.at[k], peer(0, 1, 0)
        )
        best = matched(best, source, row)
        twin_copies[k].wait_recv()
        best = matched(best, source, twin)
        lefts(source)
    top = jnp.max(best, axis=0, keepdims=True)

    lanes = 256
    per = krows // 64
    nblk = keys // 64

    def where(blk):
        c = blk // (2 * per)
        r = lax.rem(blk, 2 * per) // per
        index = (r * ncols + c) * per + lax.rem(blk, per)
        y = (index // 2).astype(jnp.float32) * coord_unit
        x = lax.rem(index, 2).astype(jnp.float32) * (64 * coord_unit)
        return x, y

    sub = lax.broadcasted_iota(jnp.int32, (8, lanes), 0).astype(jnp.float32) * coord_unit
    for q in range(0, qrows, lanes):
        cut = slice(q, q + lanes)
        tile_top = top[:, cut]

        def sums(blk, carry):
            acc, acc_x, acc_y = carry
            at = pl.ds(pl.multiple_of(blk * 64, 64), 64)
            expo = jnp.exp((score[at, cut] - tile_top) * scale)
            score[at, cut] = expo
            rows = [expo[8 * g : 8 * g + 8] for g in range(8)]
            plain = rows[0]
            tilted = rows[1] * (8 * coord_unit)
            for g in range(1, 8):
                plain = plain + rows[g]
                if g > 1:
                    tilted = tilted + rows[g] * (8 * g * coord_unit)
            x, y = where(blk)
            return acc + plain, acc_x + (tilted + plain * x), acc_y + plain * y

        zero = jnp.zeros((8, lanes), jnp.float32)
        acc, acc_x, acc_y = lax.fori_loop(0, nblk, sums, (zero, zero, zero), unroll=2)
        total = jnp.sum(acc, axis=0, keepdims=True)
        mean_x = jnp.sum(acc_x + acc * sub, axis=0, keepdims=True) / total
        mean_y = jnp.sum(acc_y, axis=0, keepdims=True) / total
        index = row * qrows + q + lax.broadcasted_iota(jnp.int32, (1, lanes), 1)
        flow_ref[0, 0:1, cut] = mean_x - (index % IMG_W).astype(jnp.float32) * coord_unit
        flow_ref[0, 1:2, cut] = mean_y - (index // IMG_W).astype(jnp.float32) * coord_unit
        cot_x = cot_ref[0, 0:1, cut]
        cot_y = cot_ref[0, 1:2, cut]
        inverse = 1.0 / total
        offset = cot_x * mean_x + cot_y * mean_y
        table[:, cut] = (
            lax.broadcasted_iota(jnp.int32, (64, lanes), 0).astype(jnp.float32) * coord_unit * cot_x
        )

        def tilt(blk, carry):
            at = pl.ds(pl.multiple_of(blk * 64, 64), 64)
            x, y = where(blk)
            base = cot_x * x + cot_y * y - offset
            prob = score[at, cut] * inverse
            slope[at, cut] = (prob * (table[:, cut] + base)).astype(jnp.bfloat16)
            return carry

        lax.fori_loop(0, nblk, tilt, 0, unroll=2)

    here = pl.ds(pl.multiple_of(col * chip + row * krows, 64), krows)
    there = pl.ds(pl.multiple_of(col * chip + twin * krows, 64), krows)
    two_out[...] = jnp.dot(slope[there, :], p1s[...], preferred_element_type=jnp.float32)
    two_copy = send(two_out, two_in, s_send.at[ncols], s_recv.at[ncols], peer(0, 1, 0))
    both = jnp.dot(left[...], slope[...], preferred_element_type=jnp.float32)
    one_t = both[:chan] * scale
    mixed = both[chan:] * scale
    term = jnp.zeros((part, chan), jnp.float32)
    for piece in pieces(mixed):
        term = term + jnp.dot(piece, p1s[...], preferred_element_type=jnp.float32)
    for piece in pieces(one_t):
        term = term + last_dims(x_one_t, piece)
    slot = pair * 2 + row
    terms[slot] = term
    term_copies = []
    for i, (dp, dr) in enumerate(group):
        term_copies.append(
            send(terms.at[slot], terms.at[slot], t_send.at[i], t_recv.at[i], peer(dp, dr, 0))
        )

    two_mine = jnp.dot(slope[here, :], p1s[...], preferred_element_type=jnp.float32)
    g1_ref[0] = last_dims(one_t.T.astype(jnp.bfloat16), weight)
    two_copy.wait_recv()
    two = (two_mine + two_in[...]) * scale
    g2_ref[0] = last_dims(two.astype(jnp.bfloat16), weight)

    for copy in term_copies:
        copy.wait_recv()
    full = terms[0]
    for i in range(1, 2 * npairs):
        full = full + terms[i]
    blocks[col] = full * (1.0 / math.sqrt(npairs * qrows * 2))
    block_copies = [
        send(blocks.at[col], blocks.at[col], b_send.at[k], b_recv.at[k], peer(0, 0, k))
        for k in range(1, ncols)
    ]
    for copy in block_copies:
        copy.wait_recv()
    gw_ref[...] = blocks[...].reshape(chan, chan)
    for copy in sends:
        copy.wait_send()


def one_kernel(npairs, ncols):
    def call(frame_one, frame_two, weight, flow_cot):
        qrows, chan = frame_one.shape[1:]
        krows = frame_two.shape[1]
        keys = krows * 2 * ncols
        part = chan // ncols
        vmem = pl.BlockSpec(memory_space=pltpu.VMEM)
        dma = pltpu.SemaphoreType.DMA
        return pl.pallas_call(
            functools.partial(fused, npairs, ncols),
            out_shape=(
                jax.ShapeDtypeStruct(flow_cot.shape, jnp.float32),
                jax.ShapeDtypeStruct(frame_one.shape, jnp.float32),
                jax.ShapeDtypeStruct(frame_two.shape, jnp.float32),
                jax.ShapeDtypeStruct(weight.shape, jnp.float32),
            ),
            in_specs=[vmem] * 4,
            out_specs=(vmem,) * 4,
            scratch_shapes=[
                pltpu.VMEM((keys, chan), jnp.bfloat16),
                pltpu.VMEM((qrows, chan), jnp.bfloat16),
                pltpu.VMEM((keys, qrows), jnp.float32),
                pltpu.VMEM((keys, qrows), jnp.bfloat16),
                pltpu.VMEM((chan + part, keys), jnp.bfloat16),
                pltpu.VMEM((64, qrows), jnp.float32),
                pltpu.VMEM((krows, chan), jnp.float32),
                pltpu.VMEM((krows, chan), jnp.float32),
                pltpu.VMEM((2 * npairs, part, chan), jnp.float32),
                pltpu.VMEM((ncols, part, chan), jnp.float32),
                dma((ncols,)),
                dma((ncols,)),
                dma((ncols + 1,)),
                dma((ncols + 1,)),
                dma((2 * npairs - 1,)),
                dma((2 * npairs - 1,)),
                dma((ncols,)),
                dma((ncols,)),
            ],
            compiler_params=pltpu.CompilerParams(
                collective_id=0, has_side_effects=True, vmem_limit_bytes=40 * 2**20
            ),
        )(frame_one, frame_two, weight, flow_cot)

    return call


def fits(mesh, frame_one, frame_two):
    npairs, nrows, ncols = (mesh.shape[name] for name in ("pairs", "rows", "cols"))
    pairs, pos, chan = frame_one.shape
    qrows = pos // nrows
    krows = pos // (nrows * ncols)
    return (
        pairs == npairs
        and nrows == 2
        and ncols > 1
        and chan % (16 * ncols) == 0
        and qrows % 256 == 0
        and krows % 64 == 0
        and IMG_W == 128
        and pos * qrows * 6 <= 24 * 2**20
    )


def solution(mesh):
    in_specs = (
        P("pairs", "rows", None),
        P("pairs", ("rows", "cols"), None),
        P(),
        P("pairs", None, "rows"),
    )
    out_specs = (
        P("pairs", None, "rows"),
        P("pairs", "rows", None),
        P("pairs", ("rows", "cols"), None),
        P(),
    )

    def program(frame_one, frame_two, weight, flow_cot):
        body = shards
        if fits(mesh, frame_one, frame_two):
            body = one_kernel(mesh.shape["pairs"], mesh.shape["cols"])
        return jax.shard_map(
            body, mesh=mesh, in_specs=in_specs, out_specs=out_specs, check_vma=False
        )(frame_one, frame_two, weight, flow_cot)

    return program
```

```python
import functools
import math

import jax
import jax.numpy as jnp
from jax import lax
from jax.experimental import pallas as pl
from jax.experimental.pallas import tpu as pltpu
from jax.sharding import PartitionSpec as P

IMG_W = 128
MESH = pl.DeviceIdType.MESH


coord_unit = 0.0625


def coords(index):
    return (
        jnp.stack([(index % IMG_W).astype(jnp.float32), (index // IMG_W).astype(jnp.float32)])
        * coord_unit
    )


def slopes(feat_q, feat_k, coord_k, top, total, cot_x, cot_y, offset, scale):
    scores = jnp.dot(feat_q, feat_k.T, preferred_element_type=jnp.float32) * scale
    prob = jnp.exp(scores - top[:, None]) / total[:, None]
    inner = cot_x[:, None] * coord_k[0][None, :] + cot_y[:, None] * coord_k[1][None, :]
    return (prob * (inner - offset[:, None])).astype(jnp.bfloat16)


def lead_product(left, right, highest):
    if highest:
        return lax.dot_general(
            left,
            right,
            (((0,), (0,)), ((), ())),
            precision=lax.Precision.HIGHEST,
            preferred_element_type=jnp.float32,
        )
    return lax.dot_general(
        left, right, (((0,), (0,)), ((), ())), preferred_element_type=jnp.float32
    )


def shards(frame_one, frame_two, weight, flow_cot):
    chan = weight.shape[0]
    scale = 1.0 / math.sqrt(chan)
    qrows = frame_one.shape[1]
    krows = frame_two.shape[1]
    nrows = lax.axis_size("rows")
    ncols = lax.axis_size("cols")
    row_id = lax.axis_index("rows")
    col_id = lax.axis_index("cols")
    x_one = frame_one[0]
    x_two = frame_two[0]
    cot = flow_cot[0]
    feat_one = jnp.dot(x_one, weight, preferred_element_type=jnp.float32).astype(jnp.bfloat16)
    feat_two = jnp.dot(x_two, weight, preferred_element_type=jnp.float32).astype(jnp.bfloat16)
    query_coords = coords(row_id * qrows + jnp.arange(qrows, dtype=jnp.int32))
    gathered = lax.all_gather(feat_two, "rows", axis=0, tiled=True)
    kcol = gathered.shape[0]
    width = min(512, kcol)
    nblk = kcol // width
    local = jnp.arange(kcol, dtype=jnp.int32)
    key_index = (local // krows * ncols + col_id) * krows + local % krows
    key_coords = coords(key_index)
    key_blocks = gathered.reshape(nblk, width, chan)
    coord_blocks = key_coords.reshape(2, nblk, width).transpose(1, 0, 2)

    def forward(carry, blk):
        top, total, sum_x, sum_y = carry
        block_keys, block_coords = blk
        scores = jnp.dot(feat_one, block_keys.T, preferred_element_type=jnp.float32) * scale
        new_top = jnp.maximum(top, jnp.max(scores, axis=1))
        shrink = jnp.exp(top - new_top)
        expo = jnp.exp(scores - new_top[:, None])
        total = total * shrink + jnp.sum(expo, axis=1)
        sum_x = sum_x * shrink + jnp.dot(expo, block_coords[0], precision=lax.Precision.HIGHEST)
        sum_y = sum_y * shrink + jnp.dot(expo, block_coords[1], precision=lax.Precision.HIGHEST)
        return ((new_top, total, sum_x, sum_y), None)

    zeros_q = jnp.zeros((qrows,), jnp.float32)
    start_carry = (jnp.full((qrows,), -1e30, jnp.float32), zeros_q, zeros_q, zeros_q)
    (top, total, sum_x, sum_y), _ = lax.scan(forward, start_carry, (key_blocks, coord_blocks))
    peak = lax.pmax(top, "cols")
    shrink = jnp.exp(top - peak)
    total, sum_x, sum_y = lax.psum((total * shrink, sum_x * shrink, sum_y * shrink), "cols")
    top = peak
    mean_x = sum_x / total
    mean_y = sum_y / total
    flow = jnp.stack([mean_x, mean_y]) - query_coords
    cot_x = cot[0]
    cot_y = cot[1]
    offset = cot_x * mean_x + cot_y * mean_y

    def backward(acc, blk):
        block_keys, block_coords = blk
        slope = slopes(feat_one, block_keys, block_coords, top, total, cot_x, cot_y, offset, scale)
        acc = acc + jnp.dot(slope, block_keys, preferred_element_type=jnp.float32) * scale
        return (acc, lead_product(slope, feat_one, False) * scale)

    part_one, terms = lax.scan(
        backward, jnp.zeros((qrows, chan), jnp.float32), (key_blocks, coord_blocks)
    )
    feat_two_grad = lax.psum_scatter(
        terms.reshape(kcol, chan), "rows", scatter_dimension=0, tiled=True
    )
    feat_one_grad = lax.psum(part_one, "cols")
    contract = (((1,), (1,)), ((), ()))
    grad_one = lax.dot_general(
        feat_one_grad.astype(jnp.bfloat16), weight, contract, preferred_element_type=jnp.float32
    )
    grad_two = lax.dot_general(
        feat_two_grad.astype(jnp.bfloat16), weight, contract, preferred_element_type=jnp.float32
    )
    term = lead_product(x_one.astype(jnp.float32), part_one, True) + lead_product(
        x_two.astype(jnp.float32), feat_two_grad, True
    )
    npairs = lax.axis_size("pairs") * frame_one.shape[0]
    grad_w = lax.psum(term, ("pairs", "rows", "cols")) / math.sqrt(npairs * qrows * nrows)
    return (flow[None], grad_one[None], grad_two[None], grad_w)


def pieces(value):
    high = value.astype(jnp.bfloat16)
    rest = value - high.astype(jnp.float32)
    mid = rest.astype(jnp.bfloat16)
    low = (rest - mid.astype(jnp.float32)).astype(jnp.bfloat16)
    return high, mid, low


def last_dims(left, right):
    return lax.dot_general(
        left, right, (((1,), (1,)), ((), ())), preferred_element_type=jnp.float32
    )


def fused(
    npairs, ncols,
    x1_hbm, x2_hbm, w_hbm, cot_hbm,
    flow_ref, g1_ref, g2_ref, gw_ref,
    x1_ref, w_ref, cot_ref, x2all, p1s, score, slope, left, table, two_out, two_in, terms, blocks,
    z_send, z_recv, s_send, s_recv, t_send, t_recv, b_send, b_recv, load_sem,
):
    qrows, chan = x1_ref.shape[1:]
    krows = x2_hbm.shape[1]
    keys = x2all.shape[0]
    chip = 2 * krows
    scale = 1.0 / math.sqrt(chan)
    pair = lax.axis_index("pairs")
    row = lax.axis_index("rows")
    col = lax.axis_index("cols")
    twin = 1 - row
    orders = [1] + [k for k in range(ncols - 1, 1, -1)]

    def peer(dp, dr, dc):
        return (lax.rem(pair + dp, npairs), lax.rem(row + dr, 2), lax.rem(col + dc, ncols))

    group = [(0, 1)] + [(dp, 0) for dp in range(1, npairs)]

    def place(c, r):
        return pl.ds(pl.multiple_of(c * chip + r * krows, 64), krows)

    own = place(col, row)
    loads = [
        pltpu.make_async_copy(src, dst, load_sem.at[i])
        for i, (src, dst) in enumerate(
            [
                (x2_hbm.at[0], x2all.at[own]),
                (w_hbm, w_ref),
                (x1_hbm, x1_ref),
                (cot_hbm, cot_ref),
            ]
        )
    ]
    for load in loads:
        load.start()
    barrier = pltpu.get_barrier_semaphore()
    for dc in range(1, ncols):
        pl.semaphore_signal(barrier, inc=1, device_id=peer(0, 0, dc), device_id_type=MESH)
    for dp, dr in group:
        pl.semaphore_signal(barrier, inc=1, device_id=peer(dp, dr, 0), device_id_type=MESH)
    loads[0].wait()
    pl.semaphore_wait(barrier, ncols - 1 + len(group))
    sends = []

    def send(src, dst, ssem, rsem, device):
        copy = pltpu.make_async_remote_copy(
            src_ref=src, dst_ref=dst, send_sem=ssem, recv_sem=rsem,
            device_id=device, device_id_type=MESH,
        )
        copy.start()
        sends.append(copy)
        return copy

    twin_copies = {0: send(x2all.at[own], x2all.at[own], s_send.at[0], s_recv.at[0], peer(0, 1, 0))}
    z_copies = {}
    for k in orders:
        z_copies[k] = send(
            x2all.at[own], x2all.at[own], z_send.at[k], z_recv.at[k], peer(0, 0, k)
        )

    for load in loads[1:]:
        load.wait()
    weight = w_ref[...]
    x_one = x1_ref[0]
    p1 = jnp.dot(x_one, weight, preferred_element_type=jnp.float32).astype(jnp.bfloat16)
    p1s[...] = p1
    pick = (
        lax.broadcasted_iota(jnp.int32, (chan, chan), 1)
        == lax.broadcasted_iota(jnp.int32, (chan, chan), 0)
    ).astype(jnp.float32)
    wt = weight.astype(jnp.float32).T
    proj = jnp.concatenate([wt, pick], axis=0).astype(jnp.bfloat16)
    x_one_t = last_dims(pick.astype(jnp.bfloat16), x_one).astype(jnp.bfloat16)

    def matched(best, c, r):
        at = place(c, r)
        feat = jnp.dot(x2all[at, :], weight, preferred_element_type=jnp.float32)
        values = last_dims(feat.astype(jnp.bfloat16), p1s[...])
        score[at, :] = values
        return jnp.maximum(best, jnp.max(values.reshape(krows // 8, 8, qrows), axis=0))

    def lefts(c):
        at = pl.ds(pl.multiple_of(c * chip, 128), chip)
        left[:, at] = last_dims(proj, x2all[at, :]).astype(jnp.bfloat16)

    best = jnp.full((8, qrows), -jnp.inf, jnp.float32)
    best = matched(best, col, row)
    twin_copies[0].wait_recv()
    best = matched(best, col, twin)
    lefts(col)
    for k in orders:
        source = lax.rem(col + ncols - k, ncols)
        at = place(source, row)
        z_copies[k].wait_recv()
        twin_copies[k] = send(
            x2all.at[at], x2all.at[at], s_send.at[k], s_recv.at[k], peer(0, 1, 0)
        )
        best = matched(best, source, row)
    for k in orders:
        source = lax.rem(col + ncols - k, ncols)
        twin_copies[k].wait_recv()
        best = matched(best, source, twin)
        lefts(source)
    top = jnp.max(best, axis=0, keepdims=True)

    lanes = 256
    per = krows // 64
    nblk = keys // 64

    def where(blk):
        c = blk // (2 * per)
        r = lax.rem(blk, 2 * per) // per
        index = (r * ncols + c) * per + lax.rem(blk, per)
        y = (index // 2).astype(jnp.float32) * coord_unit
        x = lax.rem(index, 2).astype(jnp.float32) * (64 * coord_unit)
        return x, y

    sub = lax.broadcasted_iota(jnp.int32, (8, lanes), 0).astype(jnp.float32) * coord_unit
    for q in range(0, qrows, lanes):
        cut = slice(q, q + lanes)
        tile_top = top[:, cut]

        def sums(blk, carry):
            acc, acc_x, acc_y = carry
            at = pl.ds(pl.multiple_of(blk * 64, 64), 64)
            expo = jnp.exp((score[at, cut] - tile_top) * scale)
            score[at, cut] = expo
            rows = [expo[8 * g : 8 * g + 8] for g in range(8)]
            plain = rows[0]
            tilted = rows[1] * (8 * coord_unit)
            for g in range(1, 8):
                plain = plain + rows[g]
                if g > 1:
                    tilted = tilted + rows[g] * (8 * g * coord_unit)
            x, y = where(blk)
            return acc + plain, acc_x + (tilted + plain * x), acc_y + plain * y

        zero = jnp.zeros((8, lanes), jnp.float32)
        acc, acc_x, acc_y = lax.fori_loop(0, nblk, sums, (zero, zero, zero), unroll=2)
        total = jnp.sum(acc, axis=0, keepdims=True)
        mean_x = jnp.sum(acc_x + acc * sub, axis=0, keepdims=True) / total
        mean_y = jnp.sum(acc_y, axis=0, keepdims=True) / total
        index = row * qrows + q + lax.broadcasted_iota(jnp.int32, (1, lanes), 1)
        flow_ref[0, 0:1, cut] = mean_x - (index % IMG_W).astype(jnp.float32) * coord_unit
        flow_ref[0, 1:2, cut] = mean_y - (index // IMG_W).astype(jnp.float32) * coord_unit
        cot_x = cot_ref[0, 0:1, cut]
        cot_y = cot_ref[0, 1:2, cut]
        inverse = 1.0 / total
        offset = cot_x * mean_x + cot_y * mean_y
        table[:, cut] = (
            lax.broadcasted_iota(jnp.int32, (64, lanes), 0).astype(jnp.float32) * coord_unit * cot_x
        )

        def tilt(blk, carry):
            at = pl.ds(pl.multiple_of(blk * 64, 64), 64)
            x, y = where(blk)
            base = cot_x * x + cot_y * y - offset
            prob = score[at, cut] * inverse
            slope[at, cut] = (prob * (table[:, cut] + base)).astype(jnp.bfloat16)
            return carry

        lax.fori_loop(0, nblk, tilt, 0, unroll=2)

    here = pl.ds(pl.multiple_of(col * chip + row * krows, 64), krows)
    there = pl.ds(pl.multiple_of(col * chip + twin * krows, 64), krows)
    two_out[...] = jnp.dot(slope[there, :], p1s[...], preferred_element_type=jnp.float32)
    two_copy = send(two_out, two_in, s_send.at[ncols], s_recv.at[ncols], peer(0, 1, 0))
    both = jnp.dot(left[...], slope[...], preferred_element_type=jnp.float32)
    one_t = both[:chan] * scale
    mixed = both[chan:] * scale
    term = jnp.zeros((chan, chan), jnp.float32)
    for piece in pieces(mixed):
        term = term + jnp.dot(piece, p1s[...], preferred_element_type=jnp.float32)
    for piece in pieces(one_t):
        term = term + last_dims(x_one_t, piece)
    terms[row] = term
    term_copy = send(terms.at[row], terms.at[row], t_send.at[0], t_recv.at[0], peer(0, 1, 0))
    two_mine = jnp.dot(slope[here, :], p1s[...], preferred_element_type=jnp.float32)
    term_copy.wait_recv()
    blocks[pair] = terms[0] + terms[1]
    block_copies = [
        send(blocks.at[pair], blocks.at[pair], b_send.at[k], b_recv.at[k], peer(k, 0, 0))
        for k in range(1, npairs)
    ]

    g1_ref[0] = last_dims(one_t.T.astype(jnp.bfloat16), weight)
    two_copy.wait_recv()
    two = (two_mine + two_in[...]) * scale
    g2_ref[0] = last_dims(two.astype(jnp.bfloat16), weight)

    for copy in block_copies:
        copy.wait_recv()
    full = blocks[0]
    for i in range(1, npairs):
        full = full + blocks[i]
    gw_ref[...] = full * (1.0 / math.sqrt(npairs * qrows * 2))
    for copy in sends:
        copy.wait_send()


def store(*refs):
    half = len(refs) // 2
    sem = refs[-1]
    copies = [
        pltpu.make_async_copy(src, dst, sem.at[i])
        for i, (src, dst) in enumerate(zip(refs[:half], refs[half:-1]))
    ]
    for copy in copies:
        copy.start()
    for copy in copies:
        copy.wait()


def one_kernel(npairs, ncols):
    def call(frame_one, frame_two, weight, flow_cot):
        qrows, chan = frame_one.shape[1:]
        krows = frame_two.shape[1]
        keys = krows * 2 * ncols
        vmem = pl.BlockSpec(memory_space=pltpu.VMEM)
        dma = pltpu.SemaphoreType.DMA
        hbm = pl.BlockSpec(memory_space=pltpu.HBM)
        shapes = (
            jax.ShapeDtypeStruct(flow_cot.shape, jnp.float32),
            jax.ShapeDtypeStruct(frame_one.shape, jnp.float32),
            jax.ShapeDtypeStruct(frame_two.shape, jnp.float32),
            jax.ShapeDtypeStruct(weight.shape, jnp.float32),
        )
        outs = pl.pallas_call(
            functools.partial(fused, npairs, ncols),
            out_shape=tuple(pltpu.VMEM(s.shape, s.dtype) for s in shapes),
            in_specs=[hbm] * 4,
            out_specs=(vmem,) * 4,
            scratch_shapes=[
                pltpu.VMEM(frame_one.shape, jnp.bfloat16),
                pltpu.VMEM(weight.shape, jnp.bfloat16),
                pltpu.VMEM(flow_cot.shape, jnp.float32),
                pltpu.VMEM((keys, chan), jnp.bfloat16),
                pltpu.VMEM((qrows, chan), jnp.bfloat16),
                pltpu.VMEM((keys, qrows), jnp.float32),
                pltpu.VMEM((keys, qrows), jnp.bfloat16),
                pltpu.VMEM((2 * chan, keys), jnp.bfloat16),
                pltpu.VMEM((64, qrows), jnp.float32),
                pltpu.VMEM((krows, chan), jnp.float32),
                pltpu.VMEM((krows, chan), jnp.float32),
                pltpu.VMEM((2, chan, chan), jnp.float32),
                pltpu.VMEM((npairs, chan, chan), jnp.float32),
                dma((ncols,)),
                dma((ncols,)),
                dma((ncols + 1,)),
                dma((ncols + 1,)),
                dma((1,)),
                dma((1,)),
                dma((npairs,)),
                dma((npairs,)),
                dma((4,)),
            ],
            compiler_params=pltpu.CompilerParams(
                collective_id=0, has_side_effects=True, vmem_limit_bytes=60 * 2**20
            ),
        )(frame_one, frame_two, weight, flow_cot)
        return pl.pallas_call(
            store,
            out_shape=shapes,
            in_specs=[vmem] * 4,
            out_specs=(hbm,) * 4,
            scratch_shapes=[dma((4,))],
        )(*(pltpu.with_memory_space_constraint(out, pltpu.VMEM) for out in outs))

    return call


def fits(mesh, frame_one, frame_two):
    npairs, nrows, ncols = (mesh.shape[name] for name in ("pairs", "rows", "cols"))
    pairs, pos, chan = frame_one.shape
    qrows = pos // nrows
    krows = pos // (nrows * ncols)
    return (
        pairs == npairs
        and nrows == 2
        and ncols > 1
        and chan % (16 * ncols) == 0
        and qrows % 256 == 0
        and krows % 64 == 0
        and IMG_W == 128
        and pos * qrows * 6 <= 24 * 2**20
    )


def solution(mesh):
    in_specs = (
        P("pairs", "rows", None),
        P("pairs", ("rows", "cols"), None),
        P(),
        P("pairs", None, "rows"),
    )
    out_specs = (
        P("pairs", None, "rows"),
        P("pairs", "rows", None),
        P("pairs", ("rows", "cols"), None),
        P(),
    )

    def program(frame_one, frame_two, weight, flow_cot):
        body = shards
        if fits(mesh, frame_one, frame_two):
            body = one_kernel(mesh.shape["pairs"], mesh.shape["cols"])
        return jax.shard_map(
            body, mesh=mesh, in_specs=in_specs, out_specs=out_specs, check_vma=False
        )(frame_one, frame_two, weight, flow_cot)

    return program
```

```python
import functools
import math

import jax
import jax.numpy as jnp
from jax import lax
from jax.experimental import pallas as pl
from jax.experimental.pallas import tpu as pltpu
from jax.sharding import PartitionSpec as P

IMG_W = 128
MESH = pl.DeviceIdType.MESH


coord_unit = 0.0625


def coords(index):
    return (
        jnp.stack([(index % IMG_W).astype(jnp.float32), (index // IMG_W).astype(jnp.float32)])
        * coord_unit
    )


def slopes(feat_q, feat_k, coord_k, top, total, cot_x, cot_y, offset, scale):
    scores = jnp.dot(feat_q, feat_k.T, preferred_element_type=jnp.float32) * scale
    prob = jnp.exp(scores - top[:, None]) / total[:, None]
    inner = cot_x[:, None] * coord_k[0][None, :] + cot_y[:, None] * coord_k[1][None, :]
    return (prob * (inner - offset[:, None])).astype(jnp.bfloat16)


def lead_product(left, right, highest):
    if highest:
        return lax.dot_general(
            left,
            right,
            (((0,), (0,)), ((), ())),
            precision=lax.Precision.HIGHEST,
            preferred_element_type=jnp.float32,
        )
    return lax.dot_general(
        left, right, (((0,), (0,)), ((), ())), preferred_element_type=jnp.float32
    )


def shards(frame_one, frame_two, weight, flow_cot):
    chan = weight.shape[0]
    scale = 1.0 / math.sqrt(chan)
    qrows = frame_one.shape[1]
    krows = frame_two.shape[1]
    nrows = lax.axis_size("rows")
    ncols = lax.axis_size("cols")
    row_id = lax.axis_index("rows")
    col_id = lax.axis_index("cols")
    x_one = frame_one[0]
    x_two = frame_two[0]
    cot = flow_cot[0]
    feat_one = jnp.dot(x_one, weight, preferred_element_type=jnp.float32).astype(jnp.bfloat16)
    feat_two = jnp.dot(x_two, weight, preferred_element_type=jnp.float32).astype(jnp.bfloat16)
    query_coords = coords(row_id * qrows + jnp.arange(qrows, dtype=jnp.int32))
    gathered = lax.all_gather(feat_two, "rows", axis=0, tiled=True)
    kcol = gathered.shape[0]
    width = min(512, kcol)
    nblk = kcol // width
    local = jnp.arange(kcol, dtype=jnp.int32)
    key_index = (local // krows * ncols + col_id) * krows + local % krows
    key_coords = coords(key_index)
    key_blocks = gathered.reshape(nblk, width, chan)
    coord_blocks = key_coords.reshape(2, nblk, width).transpose(1, 0, 2)

    def forward(carry, blk):
        top, total, sum_x, sum_y = carry
        block_keys, block_coords = blk
        scores = jnp.dot(feat_one, block_keys.T, preferred_element_type=jnp.float32) * scale
        new_top = jnp.maximum(top, jnp.max(scores, axis=1))
        shrink = jnp.exp(top - new_top)
        expo = jnp.exp(scores - new_top[:, None])
        total = total * shrink + jnp.sum(expo, axis=1)
        sum_x = sum_x * shrink + jnp.dot(expo, block_coords[0], precision=lax.Precision.HIGHEST)
        sum_y = sum_y * shrink + jnp.dot(expo, block_coords[1], precision=lax.Precision.HIGHEST)
        return ((new_top, total, sum_x, sum_y), None)

    zeros_q = jnp.zeros((qrows,), jnp.float32)
    start_carry = (jnp.full((qrows,), -1e30, jnp.float32), zeros_q, zeros_q, zeros_q)
    (top, total, sum_x, sum_y), _ = lax.scan(forward, start_carry, (key_blocks, coord_blocks))
    peak = lax.pmax(top, "cols")
    shrink = jnp.exp(top - peak)
    total, sum_x, sum_y = lax.psum((total * shrink, sum_x * shrink, sum_y * shrink), "cols")
    top = peak
    mean_x = sum_x / total
    mean_y = sum_y / total
    flow = jnp.stack([mean_x, mean_y]) - query_coords
    cot_x = cot[0]
    cot_y = cot[1]
    offset = cot_x * mean_x + cot_y * mean_y

    def backward(acc, blk):
        block_keys, block_coords = blk
        slope = slopes(feat_one, block_keys, block_coords, top, total, cot_x, cot_y, offset, scale)
        acc = acc + jnp.dot(slope, block_keys, preferred_element_type=jnp.float32) * scale
        return (acc, lead_product(slope, feat_one, False) * scale)

    part_one, terms = lax.scan(
        backward, jnp.zeros((qrows, chan), jnp.float32), (key_blocks, coord_blocks)
    )
    feat_two_grad = lax.psum_scatter(
        terms.reshape(kcol, chan), "rows", scatter_dimension=0, tiled=True
    )
    feat_one_grad = lax.psum(part_one, "cols")
    contract = (((1,), (1,)), ((), ()))
    grad_one = lax.dot_general(
        feat_one_grad.astype(jnp.bfloat16), weight, contract, preferred_element_type=jnp.float32
    )
    grad_two = lax.dot_general(
        feat_two_grad.astype(jnp.bfloat16), weight, contract, preferred_element_type=jnp.float32
    )
    term = lead_product(x_one.astype(jnp.float32), part_one, True) + lead_product(
        x_two.astype(jnp.float32), feat_two_grad, True
    )
    npairs = lax.axis_size("pairs") * frame_one.shape[0]
    grad_w = lax.psum(term, ("pairs", "rows", "cols")) / math.sqrt(npairs * qrows * nrows)
    return (flow[None], grad_one[None], grad_two[None], grad_w)


def pieces(value):
    high = value.astype(jnp.bfloat16)
    rest = value - high.astype(jnp.float32)
    return jnp.concatenate([high, rest.astype(jnp.bfloat16)], axis=0)


def last_dims(left, right):
    return lax.dot_general(
        left, right, (((1,), (1,)), ((), ())), preferred_element_type=jnp.float32
    )


def fused(
    npairs, ncols,
    x1_hbm, x2_hbm, w_hbm, cot_hbm,
    flow_ref, g1_ref, g2_ref, gw_ref,
    x1_ref, w_ref, cot_ref, x2all, p1s, score, slope, left, table, stats, two_out, two_in, terms, blocks,
    z_send, z_recv, s_send, s_recv, t_send, t_recv, b_send, b_recv, load_sem,
):
    qrows, chan = x1_ref.shape[1:]
    krows = x2_hbm.shape[1]
    chip = 2 * krows
    scale = 1.0 / math.sqrt(chan)
    pair = lax.axis_index("pairs")
    row = lax.axis_index("rows")
    col = lax.axis_index("cols")
    twin = 1 - row
    orders = [1] + [k for k in range(ncols - 1, 1, -1)]

    def peer(dp, dr, dc):
        return (lax.rem(pair + dp, npairs), lax.rem(row + dr, 2), lax.rem(col + dc, ncols))

    group = [(0, 1)] + [(dp, 0) for dp in range(1, npairs)]

    def place(c, r):
        return pl.ds(pl.multiple_of(c * chip + r * krows, 64), krows)

    own = place(col, row)
    loads = [
        pltpu.make_async_copy(src, dst, load_sem.at[i])
        for i, (src, dst) in enumerate(
            [
                (x2_hbm.at[0], x2all.at[own]),
                (w_hbm, w_ref),
                (x1_hbm, x1_ref),
                (cot_hbm, cot_ref),
            ]
        )
    ]
    for load in loads:
        load.start()
    barrier = pltpu.get_barrier_semaphore()
    for dc in range(1, ncols):
        pl.semaphore_signal(barrier, inc=1, device_id=peer(0, 0, dc), device_id_type=MESH)
    for dp, dr in group:
        pl.semaphore_signal(barrier, inc=1, device_id=peer(dp, dr, 0), device_id_type=MESH)
    loads[0].wait()
    pl.semaphore_wait(barrier, ncols - 1 + len(group))
    sends = []

    def send(src, dst, ssem, rsem, device):
        copy = pltpu.make_async_remote_copy(
            src_ref=src, dst_ref=dst, send_sem=ssem, recv_sem=rsem,
            device_id=device, device_id_type=MESH,
        )
        copy.start()
        sends.append(copy)
        return copy

    twin_copies = {0: send(x2all.at[own], x2all.at[own], s_send.at[0], s_recv.at[0], peer(0, 1, 0))}
    z_copies = {}
    for k in orders:
        z_copies[k] = send(
            x2all.at[own], x2all.at[own], z_send.at[k], z_recv.at[k], peer(0, 0, k)
        )

    for load in loads[1:]:
        load.wait()
    weight = w_ref[...]
    x_one = x1_ref[0]
    p1 = jnp.dot(x_one, weight, preferred_element_type=jnp.float32).astype(jnp.bfloat16)
    p1s[...] = p1
    pick = (
        lax.broadcasted_iota(jnp.int32, (chan, chan), 1)
        == lax.broadcasted_iota(jnp.int32, (chan, chan), 0)
    ).astype(jnp.float32)
    wt = weight.astype(jnp.float32).T
    proj = jnp.concatenate([wt, pick], axis=0).astype(jnp.bfloat16)

    lanes = 256
    per = krows // 64

    def where(c, blk):
        index = (blk // per * ncols + c) * per + blk % per
        if isinstance(c, int):
            return index % 2 * (64 * coord_unit), index // 2 * coord_unit
        y = (index // 2).astype(jnp.float32) * coord_unit
        x = lax.rem(index, 2).astype(jnp.float32) * (64 * coord_unit)
        return x, y

    sub = lax.broadcasted_iota(jnp.int32, (8, lanes), 0).astype(jnp.float32) * coord_unit

    def matched(c):
        at = pl.ds(pl.multiple_of(c * chip, 128), chip)
        found = x2all[at, :]
        feat = jnp.dot(found, weight, preferred_element_type=jnp.float32).astype(jnp.bfloat16)
        for q in range(0, qrows, lanes):
            cut = slice(q, q + lanes)
            values = last_dims(feat, p1s[cut, :])
            best = jnp.max(jnp.max(values.reshape(chip // 8, 8, lanes), axis=0), axis=0, keepdims=True)
            expo = jnp.exp((values - best) * scale)
            score[at, cut] = expo
            acc = acc_x = acc_y = jnp.zeros((8, lanes), jnp.float32)
            for blk in range(2 * per):
                rows = [expo[64 * blk + 8 * g : 64 * blk + 8 * g + 8] for g in range(8)]
                plain = rows[0]
                tilted = rows[1] * (8 * coord_unit)
                for g in range(1, 8):
                    plain = plain + rows[g]
                    if g > 1:
                        tilted = tilted + rows[g] * (8 * g * coord_unit)
                x, y = where(c, blk)
                acc = acc + plain
                acc_x = acc_x + (tilted + plain * x)
                acc_y = acc_y + plain * y
            stats[c, 0:1, cut] = best
            stats[c, 1:2, cut] = jnp.sum(acc, axis=0, keepdims=True)
            stats[c, 2:3, cut] = jnp.sum(acc_x + acc * sub, axis=0, keepdims=True)
            stats[c, 3:4, cut] = jnp.sum(acc_y, axis=0, keepdims=True)
        left[:, at] = last_dims(proj, found).astype(jnp.bfloat16)

    def arrive(k):
        at = place(lax.rem(col + ncols - k, ncols), row)
        z_copies[k].wait_recv()
        twin_copies[k] = send(
            x2all.at[at], x2all.at[at], s_send.at[k], s_recv.at[k], peer(0, 1, 0)
        )

    twin_copies[0].wait_recv()
    matched(col)
    arrive(orders[0])
    for i, k in enumerate(orders):
        if i + 1 < len(orders):
            arrive(orders[i + 1])
        twin_copies[k].wait_recv()
        matched(lax.rem(col + ncols - k, ncols))

    tops = [stats[c, 0:1, :] for c in range(ncols)]
    top = functools.reduce(jnp.maximum, tops)
    shrinks = [jnp.exp((part - top) * scale) for part in tops]

    def gathered(i):
        whole = stats[0, i : i + 1, :] * shrinks[0]
        for c in range(1, ncols):
            whole = whole + stats[c, i : i + 1, :] * shrinks[c]
        return whole

    total = gathered(1)
    mean_x = gathered(2) / total
    mean_y = gathered(3) / total
    index = row * qrows + lax.broadcasted_iota(jnp.int32, (1, qrows), 1)
    flow_ref[0, 0:1, :] = mean_x - (index % IMG_W).astype(jnp.float32) * coord_unit
    flow_ref[0, 1:2, :] = mean_y - (index // IMG_W).astype(jnp.float32) * coord_unit
    cot_x = cot_ref[0, 0:1, :]
    cot_y = cot_ref[0, 1:2, :]
    inverse = 1.0 / total
    offset = cot_x * mean_x + cot_y * mean_y
    table[...] = (
        lax.broadcasted_iota(jnp.int32, (64, qrows), 0).astype(jnp.float32) * coord_unit * cot_x
    )
    both = jnp.zeros((2 * chan, qrows), jnp.float32)
    for c in range(ncols):
        factor = inverse * shrinks[c]
        for blk in range(2 * per):
            at = pl.ds(c * chip + blk * 64, 64)
            x, y = where(c, blk)
            base = cot_x * x + cot_y * y - offset
            slope[at, :] = (score[at, :] * factor * (table[...] + base)).astype(jnp.bfloat16)
        at = pl.ds(c * chip, chip)
        both = both + jnp.dot(left[:, at], slope[at, :], preferred_element_type=jnp.float32)

    here = pl.ds(pl.multiple_of(col * chip + row * krows, 64), krows)
    there = pl.ds(pl.multiple_of(col * chip + twin * krows, 64), krows)
    two_out[...] = jnp.dot(slope[there, :], p1s[...], preferred_element_type=jnp.float32)
    two_copy = send(two_out, two_in, s_send.at[ncols], s_recv.at[ncols], peer(0, 1, 0))
    one_t = both[:chan] * scale
    mixed = both[chan:] * scale
    by_two = jnp.dot(pieces(mixed), p1s[...], preferred_element_type=jnp.float32)
    by_one = jnp.dot(pieces(one_t), x1_ref[0], preferred_element_type=jnp.float32)
    term = by_two[:chan] + by_two[chan:] + (by_one[:chan] + by_one[chan:]).T
    terms[row] = term
    term_copy = send(terms.at[row], terms.at[row], t_send.at[0], t_recv.at[0], peer(0, 1, 0))
    two_mine = jnp.dot(slope[here, :], p1s[...], preferred_element_type=jnp.float32)
    term_copy.wait_recv()
    blocks[pair] = terms[0] + terms[1]
    block_copies = [
        send(blocks.at[pair], blocks.at[pair], b_send.at[k], b_recv.at[k], peer(k, 0, 0))
        for k in range(1, npairs)
    ]

    g1_ref[0] = last_dims(one_t.T.astype(jnp.bfloat16), weight)
    two_copy.wait_recv()
    two = (two_mine + two_in[...]) * scale
    g2_ref[0] = last_dims(two.astype(jnp.bfloat16), weight)

    for copy in block_copies:
        copy.wait_recv()
    full = blocks[0]
    for i in range(1, npairs):
        full = full + blocks[i]
    gw_ref[...] = full * (1.0 / math.sqrt(npairs * qrows * 2))
    for copy in sends:
        copy.wait_send()


def store(*refs):
    half = len(refs) // 2
    sem = refs[-1]
    copies = [
        pltpu.make_async_copy(src, dst, sem.at[i])
        for i, (src, dst) in enumerate(zip(refs[:half], refs[half:-1]))
    ]
    for copy in copies:
        copy.start()
    for copy in copies:
        copy.wait()


def one_kernel(npairs, ncols):
    def call(frame_one, frame_two, weight, flow_cot):
        qrows, chan = frame_one.shape[1:]
        krows = frame_two.shape[1]
        keys = krows * 2 * ncols
        vmem = pl.BlockSpec(memory_space=pltpu.VMEM)
        dma = pltpu.SemaphoreType.DMA
        hbm = pl.BlockSpec(memory_space=pltpu.HBM)
        shapes = (
            jax.ShapeDtypeStruct(flow_cot.shape, jnp.float32),
            jax.ShapeDtypeStruct(frame_one.shape, jnp.float32),
            jax.ShapeDtypeStruct(frame_two.shape, jnp.float32),
            jax.ShapeDtypeStruct(weight.shape, jnp.float32),
        )
        outs = pl.pallas_call(
            functools.partial(fused, npairs, ncols),
            out_shape=tuple(pltpu.VMEM(s.shape, s.dtype) for s in shapes),
            in_specs=[hbm] * 4,
            out_specs=(vmem,) * 4,
            scratch_shapes=[
                pltpu.VMEM(frame_one.shape, jnp.bfloat16),
                pltpu.VMEM(weight.shape, jnp.bfloat16),
                pltpu.VMEM(flow_cot.shape, jnp.float32),
                pltpu.VMEM((keys, chan), jnp.bfloat16),
                pltpu.VMEM((qrows, chan), jnp.bfloat16),
                pltpu.VMEM((keys, qrows), jnp.float32),
                pltpu.VMEM((keys, qrows), jnp.bfloat16),
                pltpu.VMEM((2 * chan, keys), jnp.bfloat16),
                pltpu.VMEM((64, qrows), jnp.float32),
                pltpu.VMEM((ncols, 8, qrows), jnp.float32),
                pltpu.VMEM((krows, chan), jnp.float32),
                pltpu.VMEM((krows, chan), jnp.float32),
                pltpu.VMEM((2, chan, chan), jnp.float32),
                pltpu.VMEM((npairs, chan, chan), jnp.float32),
                dma((ncols,)),
                dma((ncols,)),
                dma((ncols + 1,)),
                dma((ncols + 1,)),
                dma((1,)),
                dma((1,)),
                dma((npairs,)),
                dma((npairs,)),
                dma((4,)),
            ],
            compiler_params=pltpu.CompilerParams(
                collective_id=0, has_side_effects=True, vmem_limit_bytes=60 * 2**20
            ),
        )(frame_one, frame_two, weight, flow_cot)
        return pl.pallas_call(
            store,
            out_shape=shapes,
            in_specs=[vmem] * 4,
            out_specs=(hbm,) * 4,
            scratch_shapes=[dma((4,))],
        )(*(pltpu.with_memory_space_constraint(out, pltpu.VMEM) for out in outs))

    return call


def fits(mesh, frame_one, frame_two):
    npairs, nrows, ncols = (mesh.shape[name] for name in ("pairs", "rows", "cols"))
    pairs, pos, chan = frame_one.shape
    qrows = pos // nrows
    krows = pos // (nrows * ncols)
    return (
        pairs == npairs
        and nrows == 2
        and ncols > 1
        and chan % (16 * ncols) == 0
        and qrows % 256 == 0
        and krows % 64 == 0
        and qrows % IMG_W == 0
        and IMG_W == 128
        and pos * qrows * 6 <= 24 * 2**20
    )


def solution(mesh):
    in_specs = (
        P("pairs", "rows", None),
        P("pairs", ("rows", "cols"), None),
        P(),
        P("pairs", None, "rows"),
    )
    out_specs = (
        P("pairs", None, "rows"),
        P("pairs", "rows", None),
        P("pairs", ("rows", "cols"), None),
        P(),
    )

    def program(frame_one, frame_two, weight, flow_cot):
        body = shards
        if fits(mesh, frame_one, frame_two):
            body = one_kernel(mesh.shape["pairs"], mesh.shape["cols"])
        return jax.shard_map(
            body, mesh=mesh, in_specs=in_specs, out_specs=out_specs, check_vma=False
        )(frame_one, frame_two, weight, flow_cot)

    return program
```
